32 devices in a mesh: dp: 8 (over z, y), fsdp: 4 (over x, core).
Axes of the slice: x: 2, y: 2, z: 4, core: 2. Of those that a mesh axis runs over, the one named last changes fastest.
Arguments:
- tokens: bfloat16 [4096, 1024], P(('dp', 'fsdp')), may hold values from -6 to 6
- cotangent: bfloat16 [4096, 1024], P(('dp', 'fsdp')), may hold values from -6 to 6
- tile_len: int32 [128], P(('dp', 'fsdp')), may hold values from 0 to 32, as said below
- tile_join: int32 [128], P(('dp', 'fsdp')), may hold values from 0 to 1, as said below
- w_qkv: float32 [1024, 3072], P(('dp', 'fsdp')), may hold values from -0.25 to 0.25
- w_out: float32 [1024, 1024], P(('dp', 'fsdp')), may hold values from -0.5 to 0.5
- w_up: float32 [1024, 4096], P(('dp', 'fsdp')), may hold values from -0.1875 to 0.1875
- w_down: float32 [1024, 4096], P(('dp', 'fsdp')), may hold values from -0.09375 to 0.09375
- vectors: float32 [12, 1024], P(None, ('dp', 'fsdp')), as said below
- state_qkv: float32 [2, 1024, 3072], P(None, ('dp', 'fsdp')), as said below
- state_out: float32 [2, 1024, 1024], P(None, ('dp', 'fsdp')), as said below
- state_up: float32 [2, 1024, 4096], P(None, ('dp', 'fsdp')), as said below
- state_down: float32 [2, 1024, 4096], P(None, ('dp', 'fsdp')), as said below
- state_vectors: float32 [2, 12, 1024], P(None, None, ('dp', 'fsdp')), as said below
Outputs:
- activations: bfloat16 [4096, 1024], P(('dp', 'fsdp'))
- input_grad: float32 [4096, 1024], P(('dp', 'fsdp'))
- grad_w_qkv: float32 [1024, 3072], P(('dp', 'fsdp'))
- grad_w_out: float32 [1024, 1024], P(('dp', 'fsdp'))
- grad_w_up: float32 [1024, 4096], P(('dp', 'fsdp'))
- grad_w_down: float32 [1024, 4096], P(('dp', 'fsdp'))
- grad_vectors: float32 [12, 1024], P(None, ('dp', 'fsdp'))
- new_state_qkv: float32 [2, 1024, 3072], P(None, ('dp', 'fsdp'))
- new_state_out: float32 [2, 1024, 1024], P(None, ('dp', 'fsdp'))
- new_state_up: float32 [2, 1024, 4096], P(None, ('dp', 'fsdp'))
- new_state_down: float32 [2, 1024, 4096], P(None, ('dp', 'fsdp'))
- new_state_vectors: float32 [2, 12, 1024], P(None, None, ('dp', 'fsdp'))
- new_w_qkv: float32 [1024, 3072], P(('dp', 'fsdp'))
- new_w_out: float32 [1024, 1024], P(('dp', 'fsdp'))
- new_w_up: float32 [1024, 4096], P(('dp', 'fsdp'))
- new_w_down: float32 [1024, 4096], P(('dp', 'fsdp'))
- new_vectors: float32 [12, 1024], P(None, ('dp', 'fsdp'))
The draws below stay inside these ranges and needn't reach their ends.
Inputs may be any that keep to these rules, and one draw needn't show every extreme that they name: `tile_len`: a tile whose tile_join is 1 has at least one valid row, and the tile before it has 32. `tile_join`: the first tile of each block of 2 tiles has 0. `vectors`: rows 0 and 5 are gains near 1, the others biases. `state_qkv`: index 0 holds first moments, index 1 second moments, which are positive. `state_out`: as state_qkv. `state_up`: as state_qkv. `state_down`: as state_qkv. `state_vectors`: as state_qkv.
All inputs are finite; a program needn't handle non-finite values.
Results may differ from the reference program's by a relative error of at most 0.012.
The reference program's roundings to bfloat16 on the way count: a program that leaves them out, or rounds other values in their place, can miss the bound.
Values may be sent and summed in bfloat16 or wider, within the bound.
A program may use at most 256 MiB of HBM per device.

```python
import math
import jax
import jax.numpy as jnp
from jax import lax

D = 1024
H = 16
HD = 64
FF = 4096
TILE = 32
TPM = 2
STEP = 10
TOKENS = 4096


def tile_plan(key):
    tile_count = TOKENS // TILE
    full_key, length_key, join_key = jax.random.split(key, 3)
    full_flags = jax.random.randint(full_key, (tile_count,), 0, 2).astype(jnp.int32)
    partial_value = jax.random.randint(length_key, (tile_count,), 0, TILE).astype(jnp.int32)
    coin_flip = jax.random.randint(join_key, (tile_count,), 0, 5).astype(jnp.int32)
    first_tile = jnp.arange(tile_count, dtype=jnp.int32) % TPM == 0
    previous_full = jnp.concatenate([jnp.zeros((1,), jnp.int32), full_flags[:-1]])
    join_flags = jnp.where(first_tile, 0, jnp.where(previous_full == 1, (coin_flip < 3).astype(jnp.int32), 0)).astype(jnp.int32)
    tile_lengths = jnp.where(full_flags == 1, TILE, jnp.maximum(partial_value, join_flags)).astype(jnp.int32)
    return (tile_lengths, join_flags)


def draw_tile_len(key, part):
    return tile_plan(key)[0]


def draw_tile_join(key, part):
    return tile_plan(key)[1]


def draw_vectors(key, part):
    key = jax.random.fold_in(key, 7)
    gain_key, shift_key = jax.random.split(key)
    gains = jax.random.uniform(gain_key, (12, D), jnp.float32, 0.6, 1.4)
    shifts = 0.3 * jax.random.normal(shift_key, (12, D), jnp.float32)
    row_ids = jnp.arange(12, dtype=jnp.int32)
    is_gain = (row_ids == 0) | (row_ids == 5)
    return jnp.where(is_gain[:, None], gains, shifts).astype(jnp.float32)


def moment_pair(key, shape, scale):
    sign_key, first_key, second_key = jax.random.split(key, 3)
    sign_flip = jnp.where(jax.random.bernoulli(sign_key, 0.5, shape), 1.0, -1.0)
    first_size = jnp.exp(jax.random.uniform(first_key, shape, jnp.float32, jnp.log(0.5), jnp.log(2.0)))
    second_size = jnp.exp(jax.random.uniform(second_key, shape, jnp.float32, jnp.log(0.5), jnp.log(8.0)))
    first_moment = 0.111 * scale * sign_flip * first_size
    second_moment = 0.001 * scale * scale * second_size
    return jnp.stack([first_moment, second_moment]).astype(jnp.float32)


def grad_size(factor):
    return factor * (0.75 * TOKENS) ** 0.5


def draw_state_qkv(key, part):
    key = jax.random.fold_in(key, 11)
    return moment_pair(key, (D, 3 * D), grad_size(0.3))


def draw_state_out(key, part):
    key = jax.random.fold_in(key, 13)
    return moment_pair(key, (D, D), grad_size(0.35))


def draw_state_up(key, part):
    key = jax.random.fold_in(key, 17)
    return moment_pair(key, (D, FF), grad_size(0.3))


def draw_state_down(key, part):
    key = jax.random.fold_in(key, 19)
    return moment_pair(key, (D, FF), grad_size(0.5))


def draw_state_vectors(key, part):
    key = jax.random.fold_in(key, 23)
    return moment_pair(key, (12, D), grad_size(0.5))


def spiked(values, own_key, source, target, parts, factor):
    owner, partner = [(jnp.arange(values.shape[position]) // (values.shape[position] // parts)).reshape([-1 if axis == position else 1 for axis in range(values.ndim)]) for position in (source, target)]
    chosen = jax.random.permutation(own_key, parts)[partner]
    strong = (owner == chosen) | (owner == (partner + parts // 2) % parts)
    return jnp.where(strong, factor * values, values)


def block_scale(stream_key, dims, cuts, low, largest):
    loudness = 1.0
    for dim, parts in cuts:
        steps = jax.random.uniform(jax.random.fold_in(jax.random.fold_in(stream_key, 6), dim), (parts,), jnp.float32, low / len(cuts), largest / len(cuts))
        loudness = loudness * jnp.repeat(jnp.exp(steps), dims[dim] // parts).reshape((-1,) + (1,) * (len(dims) - 1 - dim))
    return loudness


def centred(key, dims, scale, bound, cuts=(), held_as=jnp.bfloat16):
    loudness = block_scale(key, dims, cuts, -0.22, 0.18) if cuts else 1.0
    drawn = jax.random.normal(key, dims, jnp.float32) * scale * loudness
    return jnp.minimum(jnp.maximum(drawn, -bound), bound).astype(held_as)


def bell_draw_with(own_key, shape, scale, reach, cuts, heavy, kind=jnp.bfloat16):
    values = scale * jax.random.normal(own_key, shape, jnp.float32)
    if cuts:
        values = values * block_scale(own_key, shape, cuts, -0.22, 0.18)
    return jnp.clip(spiked(values, jax.random.fold_in(own_key, 3), *heavy), -reach, reach).astype(kind)


def setup_inputs(seed: int = 0) -> dict:
    splits = jax.random.split(jax.random.key(seed), 15)
    tokens = bell_draw_with(splits[0], (TOKENS, D), 1.0, 6.0, ((0, 32),), (0, 1, 32, 2.75))
    cotangent = bell_draw_with(splits[1], (TOKENS, D), 1.0, 6.0, ((0, 32),), (0, 1, 32, 2.75))
    tile_len = draw_tile_len(jax.random.fold_in(splits[14], 71), 0)
    tile_join = draw_tile_join(jax.random.fold_in(splits[14], 71), 0)
    w_qkv = centred(splits[4], (D, 3 * D), (D // 2) ** -0.5, 0.25, ((0, 32),), jnp.float32)
    w_out = centred(splits[5], (D, D), (D // 8) ** -0.5, 0.5, ((0, 32),), jnp.float32)
    w_up = centred(splits[6], (D, FF), D ** -0.5, 0.1875, ((0, 32),), jnp.float32)
    w_down = centred(splits[7], (D, FF), FF ** -0.5, 0.09375, ((0, 32),), jnp.float32)
    vectors = draw_vectors(jax.random.fold_in(splits[14], 71), 0)
    state_qkv = draw_state_qkv(jax.random.fold_in(splits[14], 71), 0)
    state_out = draw_state_out(jax.random.fold_in(splits[14], 71), 0)
    state_up = draw_state_up(jax.random.fold_in(splits[14], 71), 0)
    state_down = draw_state_down(jax.random.fold_in(splits[14], 71), 0)
    state_vectors = draw_state_vectors(jax.random.fold_in(splits[14], 71), 0)
    return dict(tokens=tokens, cotangent=cotangent, tile_len=tile_len, tile_join=tile_join, w_qkv=w_qkv, w_out=w_out, w_up=w_up, w_down=w_down, vectors=vectors, state_qkv=state_qkv, state_out=state_out, state_up=state_up, state_down=state_down, state_vectors=state_vectors)


@jax.custom_vjp
def low(v):
    return lax.optimization_barrier(v.astype(jnp.bfloat16)).astype(jnp.float32)

@jax.custom_vjp
def low_back(v):
    return v

def low_keep(v):
    return (low(v), None)

def low_pass(kept, grad):
    return (grad,)

def back_keep(v):
    return (v, None)

def back_low(kept, grad):
    return (low(grad),)
low.defvjp(low_keep, low_pass)
low_back.defvjp(back_keep, back_low)
rate_matrix = 0.06
rate_vector = 1.0
decay_matrix = 0.1

def product(left_side, right_side):
    return jnp.dot(left_side, right_side, precision=lax.Precision.HIGHEST)

def layer_norm(values, gain_row, shift_row):
    centre = values - lax.optimization_barrier(jnp.mean(values, axis=-1, keepdims=True))
    spread = lax.optimization_barrier(jnp.mean(centre * centre, axis=-1, keepdims=True))
    return centre * lax.rsqrt(spread + 1e-05) * gain_row + shift_row

def tile_masks(lengths, join_flags):
    sequence_ids = jnp.cumsum((1 - join_flags).astype(jnp.int32), axis=-1).astype(jnp.int32)
    places = jnp.arange(TILE, dtype=jnp.int32)
    valid_rows = places < lengths[..., None]
    owner_ids = jnp.broadcast_to(sequence_ids[..., None], valid_rows.shape)
    shape_rows = lengths.shape[:-1] + (TPM * TILE,)
    return (valid_rows.reshape(shape_rows), owner_ids.reshape(shape_rows))

def allowed_pairs(valid_rows, owner_ids):
    places = jnp.arange(valid_rows.shape[-1], dtype=jnp.int32)
    causal = places[:, None] >= places[None, :]
    same_seq = owner_ids[:, None] == owner_ids[None, :]
    both_valid = valid_rows[:, None] & valid_rows[None, :]
    return causal & same_seq & both_valid | (places[:, None] == places[None, :])

def attend(entry):
    query_rows, key_rows, value_rows, valid_rows, owner_ids = entry
    row_count = query_rows.shape[0]
    query_heads = query_rows.reshape(row_count, H, HD)
    key_heads = key_rows.reshape(row_count, H, HD)
    value_heads = value_rows.reshape(row_count, H, HD)
    scores = jnp.einsum('qhd,khd->hqk', query_heads, key_heads, precision=lax.Precision.HIGHEST) * HD ** (-0.5)
    scores = low_back(scores)
    scores = jnp.where(allowed_pairs(valid_rows, owner_ids)[None], scores, -1000000000.0)
    probabilities = low(jax.nn.softmax(scores, axis=-1))
    attended = jnp.einsum('hqk,khd->qhd', probabilities, value_heads, precision=lax.Precision.HIGHEST)
    return attended.reshape(row_count, H * HD)

def forward(inputs, weight_qkv, weight_out, weight_up, weight_down, vector_rows, valid_rows, owner_ids):
    block_count = valid_rows.shape[0]
    normed_one = low(layer_norm(inputs, vector_rows[0], vector_rows[1]))
    bias_qkv = jnp.concatenate([vector_rows[2], jnp.zeros_like(vector_rows[2]), vector_rows[3]])
    qkv = low(low_back(product(normed_one, weight_qkv) + bias_qkv))
    shaped = qkv.reshape(block_count, TPM * TILE, 3, D)
    attended = lax.map(jax.checkpoint(attend), (shaped[:, :, 0], shaped[:, :, 1], shaped[:, :, 2], valid_rows, owner_ids))
    attended = low(low_back(attended.reshape(-1, D)))
    middle = inputs + low_back(product(attended, weight_out.T) + vector_rows[4])
    normed_two = low(layer_norm(middle, vector_rows[5], vector_rows[6]))
    hidden = low_back(product(normed_two, weight_up) + vector_rows[8:12].reshape(-1))
    active = low(jax.nn.gelu(hidden, approximate=True))
    return middle + low_back(product(active, weight_down.T) + vector_rows[7])

def adamw(master, gradient, moments, step_rate, decay_rate):
    first_moment = 0.9 * moments[0] + 0.1 * gradient
    second_moment = 0.999 * moments[1] + 0.001 * gradient * gradient
    first_hat = first_moment / (1.0 - 0.9 ** STEP)
    second_hat = second_moment / (1.0 - 0.999 ** STEP)
    updated = master - step_rate * (first_hat / (jnp.sqrt(second_hat) + 1e-08) + decay_rate * master)
    return (jnp.stack([first_moment, second_moment]), updated)

def reference(tokens, cotangent, tile_len, tile_join, w_qkv, w_out, w_up, w_down, vectors, state_qkv, state_out, state_up, state_down, state_vectors):
    masters = (w_qkv, w_out, w_up, w_down, vectors)
    rounded = tuple((low(master) for master in masters))
    block_rows = TPM * TILE
    block_total = TOKENS // block_rows
    group_blocks = math.gcd(block_total, 16)
    group_count = block_total // group_blocks
    token_groups = tokens.astype(jnp.float32).reshape(group_count, group_blocks * block_rows, D)
    cot_groups = cotangent.astype(jnp.float32).reshape(group_count, group_blocks * block_rows, D)
    length_groups = tile_len.reshape(group_count, group_blocks, TPM)
    join_groups = tile_join.reshape(group_count, group_blocks, TPM)

    def pass_group(carry, entry):
        inputs, cot_rows, lengths, join_flags = entry
        valid_rows, owner_ids = tile_masks(lengths, join_flags)

        def run_block(values, weight_qkv, weight_out, weight_up, weight_down, vector_rows):
            return forward(values, weight_qkv, weight_out, weight_up, weight_down, vector_rows, valid_rows, owner_ids)
        result, pull = jax.vjp(run_block, inputs, *rounded)
        grads = pull(cot_rows * valid_rows.reshape(-1, 1).astype(jnp.float32))
        carry = tuple((total_grad + new_grad for total_grad, new_grad in zip(carry, grads[1:])))
        return (carry, (result.astype(jnp.bfloat16), grads[0]))
    zero_grads = tuple((jnp.zeros_like(master) for master in masters))
    totals, (results, input_grads) = lax.scan(pass_group, zero_grads, (token_groups, cot_groups, length_groups, join_groups))
    activations = results.reshape(TOKENS, D)
    input_grad = input_grads.reshape(TOKENS, D)
    states = (state_qkv, state_out, state_up, state_down, state_vectors)
    step_rates = (rate_matrix, rate_matrix, rate_matrix, rate_matrix, rate_vector)
    decay_rates = (decay_matrix, decay_matrix, decay_matrix, decay_matrix, 0.0)
    updates = [adamw(masters[place], totals[place], states[place], step_rates[place], decay_rates[place]) for place in range(5)]
    return (activations, input_grad, totals[0], totals[1], totals[2], totals[3], totals[4], updates[0][0], updates[1][0], updates[2][0], updates[3][0], updates[4][0], updates[0][1], updates[1][1], updates[2][1], updates[3][1], updates[4][1])
```

```python
import functools

import jax
import jax.numpy as jnp
from jax import lax
from jax.experimental import pallas as pl
from jax.experimental.pallas import tpu as pltpu
from jax.sharding import PartitionSpec as P

D = 1024
HD = 64
FF = 4096
TILE = 32
TPM = 2
STEP = 10
BLOCK = TPM * TILE
EPS = 1e-05
VEC_PAD = 128
SCALE = HD**-0.5

rate_matrix = 0.06
rate_vector = 1.0
decay_matrix = 0.1

BF = jnp.bfloat16
F32 = jnp.float32
NN = (((1,), (0,)), ((), ()))
NT = (((1,), (1,)), ((), ()))
TN = (((0,), (0,)), ((), ()))


def dot(left, right, dims=NN):
    return lax.dot_general(left, right, dims, preferred_element_type=F32)


def normalize(values):
    centre = values - jnp.mean(values, axis=-1, keepdims=True)
    spread = jnp.mean(centre * centre, axis=-1, keepdims=True)
    inverse = lax.rsqrt(spread + EPS)
    return centre * inverse, inverse


def norm_backward(grads, gain, normed, inverse):
    scaled = grads * gain
    return inverse * (
        scaled
        - jnp.mean(scaled, axis=-1, keepdims=True)
        - normed * jnp.mean(scaled * normed, axis=-1, keepdims=True)
    )


def gelu_and_slope(values):
    root = (2.0 / jnp.pi) ** 0.5
    square = values * values
    bent = jnp.tanh(root * values * (1.0 + 0.044715 * square))
    half = 0.5 * (1.0 + bent)
    slope = half + 0.5 * values * (1.0 - bent * bent) * root * (1.0 + 3 * 0.044715 * square)
    return values * half, slope


def probabilities(query, key, mask):
    scores = jnp.where(mask, dot(query, key, NT) * SCALE, -1000000000.0)
    exp_scores = jnp.exp(scores - jnp.max(scores, axis=-1, keepdims=True))
    return exp_scores / jnp.sum(exp_scores, axis=-1, keepdims=True)


def attend_kernel(width, qkv_ref, mask_ref, out_ref):
    mask = mask_ref[...] > 0.5
    heads = []
    for at in range(0, width, HD):
        query = qkv_ref[:, at : at + HD]
        key = qkv_ref[:, width + at : width + at + HD]
        value = qkv_ref[:, 2 * width + at : 2 * width + at + HD]
        probs = probabilities(query, key, mask).astype(BF)
        heads.append(dot(probs, value))
    out_ref[...] = jnp.concatenate(heads, axis=1).astype(BF)


def attend_back_kernel(width, qkv_ref, mask_ref, grad_ref, out_ref):
    mask = mask_ref[...] > 0.5
    grad_q, grad_k, grad_v = [], [], []
    for at in range(0, width, HD):
        query = qkv_ref[:, at : at + HD]
        key = qkv_ref[:, width + at : width + at + HD]
        value = qkv_ref[:, 2 * width + at : 2 * width + at + HD]
        grad = grad_ref[:, at : at + HD]
        probs = probabilities(query, key, mask)
        grad_probs = dot(grad, value, NT)
        inner = jnp.sum(grad_probs * probs, axis=-1, keepdims=True)
        grad_scores = (probs * (grad_probs - inner)).astype(BF)
        grad_q.append(dot(grad_scores, key) * SCALE)
        grad_k.append(dot(grad_scores, query, TN) * SCALE)
        grad_v.append(dot(probs.astype(BF), grad, TN))
    out_ref[...] = jnp.concatenate(grad_q + grad_k + grad_v, axis=1).astype(BF)


def attention_call(kernel, own, width, out_width, name, *operands):
    total = operands[0].shape[0]
    return pl.pallas_call(
        functools.partial(kernel, width),
        grid=(total // own,),
        in_specs=[pl.BlockSpec((own, item.shape[1]), lambda i: (i, 0)) for item in operands],
        out_specs=pl.BlockSpec((own, out_width), lambda i: (i, 0)),
        out_shape=jax.ShapeDtypeStruct((total, out_width), BF),
        compiler_params=pltpu.CompilerParams(vmem_limit_bytes=32 * 1024 * 1024),
        name=name,
    )(*operands)


def row_codes(lengths, joins):
    per_block = joins.reshape(-1, TPM)
    sequence = jnp.cumsum(1 - per_block, axis=1)
    block = jnp.arange(per_block.shape[0], dtype=jnp.int32)[:, None]
    owner = (block * (TPM + 1) + sequence).reshape(-1)
    places = jnp.arange(TILE, dtype=jnp.int32)
    valid = (places[None, :] < lengths[:, None]).reshape(-1)
    codes = jnp.repeat(owner, TILE)
    rows = jnp.arange(codes.shape[0], dtype=jnp.int32)
    return valid, jnp.where(valid, codes, -1 - rows)


def gather_rows(values, ways):
    pieces = [values]
    for step in range(1, ways):
        order = [(place, (place + step) % ways) for place in range(ways)]
        pieces.append(lax.ppermute(values, "fsdp", order))
    return jnp.concatenate(pieces, axis=0)


def sum_rows(partial, ways):
    own = partial.shape[0] // ways
    total = partial[:own]
    for step in range(1, ways):
        order = [(place, (place - step) % ways) for place in range(ways)]
        piece = partial[step * own : (step + 1) * own].astype(BF)
        total = total + lax.ppermute(piece, "fsdp", order).astype(F32)
    return total


def exchange(values):
    return lax.all_to_all(values, "fsdp", split_axis=0, concat_axis=0, tiled=True)


def adamw(master, gradient, moments, step_rate, decay_rate):
    first_moment = 0.9 * moments[0] + 0.1 * gradient
    second_moment = 0.999 * moments[1] + 0.001 * gradient * gradient
    first_hat = first_moment / (1.0 - 0.9**STEP)
    second_hat = second_moment / (1.0 - 0.999**STEP)
    updated = master - step_rate * (
        first_hat / (jnp.sqrt(second_hat) + 1e-08) + decay_rate * master
    )
    return (jnp.stack([first_moment, second_moment]), updated)


def column_parts(weight, ways):
    rows = weight.shape[0]
    return weight.astype(BF).reshape(rows, ways, -1).transpose(1, 0, 2)


def column_whole(parts):
    return parts.transpose(1, 0, 2).reshape(parts.shape[1], -1)


def per_device(
    ways,
    tokens,
    cotangent,
    tile_len,
    tile_join,
    w_qkv,
    w_out,
    w_up,
    w_down,
    vectors,
    state_qkv,
    state_out,
    state_up,
    state_down,
    state_vectors,
):
    masters = (w_qkv, w_out, w_up, w_down, vectors)
    rows_own = w_qkv.shape[0]
    own = tokens.shape[0]
    width = D // ways
    hidden_width = FF // ways
    me = lax.axis_index("fsdp")

    with jax.named_scope("weights"):
        qkv_parts = (
            w_qkv.astype(BF).reshape(rows_own, 3, ways, width).transpose(2, 0, 1, 3)
        ).reshape(ways, rows_own, 3 * width)
        vector_part = jnp.pad(vectors.T, ((0, 0), (0, VEC_PAD - vectors.shape[0]))).astype(BF)
        first_payload = jnp.concatenate(
            [
                qkv_parts,
                column_parts(w_out, ways),
                jnp.broadcast_to(vector_part[None], (ways, rows_own, VEC_PAD)),
            ],
            axis=2,
        )
        second_payload = jnp.concatenate(
            [column_parts(w_up, ways), column_parts(w_down, ways)], axis=2
        )
        first_rows = exchange(first_payload).reshape(ways * rows_own, -1)
        first_weights = lax.all_gather(first_rows, "dp", axis=0, tiled=True)
        second_rows = exchange(second_payload).reshape(ways * rows_own, -1)
        second_weights = lax.all_gather(second_rows, "dp", axis=0, tiled=True)

    with jax.named_scope("rows"):
        valid, codes = row_codes(tile_len, tile_join)
        grad_branch = jnp.where(valid[:, None], cotangent, jnp.zeros_like(cotangent))
        all_tokens = gather_rows(tokens, ways)
        all_branch = gather_rows(grad_branch, ways)
        all_codes = gather_rows(codes, ways).reshape(ways, own)
        places = jnp.arange(own, dtype=jnp.int32)
        causal = places[:, None] >= places[None, :]
        mask = (all_codes[:, :, None] == all_codes[:, None, :]) & causal[None]
        mask = mask.astype(F32).reshape(ways * own, own)

    weight_qkv = first_weights[:, : 3 * width]
    weight_out = first_weights[:, 3 * width : 4 * width]
    vector_rows = first_weights[:, 4 * width : 4 * width + vectors.shape[0]].T.astype(F32)
    bias_query = lax.dynamic_slice(vector_rows[2], (me * width,), (width,))
    bias_value = lax.dynamic_slice(vector_rows[3], (me * width,), (width,))
    bias_qkv = jnp.concatenate([bias_query, jnp.zeros_like(bias_query), bias_value])
    bias_up = lax.dynamic_slice(
        vector_rows[8:12].reshape(-1), (me * hidden_width,), (hidden_width,)
    )

    with jax.named_scope("forward"):
        inputs = tokens.astype(F32)
        all_normed, _ = normalize(all_tokens.astype(F32))
        first_in = (all_normed * vector_rows[0] + vector_rows[1]).astype(BF)
        qkv = (dot(first_in, weight_qkv) + bias_qkv).astype(BF)
        attended = attention_call(attend_kernel, own, width, width, "attend", qkv, mask)
        out_terms = sum_rows(dot(attended, weight_out, NT), ways)
        middle = inputs + out_terms + vector_rows[4]
        normed_two, inverse_two = normalize(middle)
        second_own = (normed_two * vector_rows[5] + vector_rows[6]).astype(BF)
        second_in = gather_rows(second_own, ways)

    weight_up = second_weights[:, :hidden_width]
    weight_down = second_weights[:, hidden_width:]

    with jax.named_scope("branch"):
        hidden = dot(second_in, weight_up) + bias_up
        active, slope = gelu_and_slope(hidden)
        active = active.astype(BF)
        grad_hidden = (dot(all_branch, weight_down) * slope).astype(BF)
        second_terms = sum_rows(dot(grad_hidden, weight_up, NT), ways)

    with jax.named_scope("branch_sums"):
        branch_grads = jnp.concatenate(
            [dot(second_in, grad_hidden, TN), dot(all_branch, active, TN)], axis=1
        )
        branch_total = lax.psum_scatter(branch_grads, "dp", scatter_dimension=0, tiled=True)

    with jax.named_scope("backward"):
        grad_result = grad_branch.astype(F32)
        grad_middle = grad_result + norm_backward(
            second_terms, vector_rows[5], normed_two, inverse_two
        )
        grad_attn = grad_middle.astype(BF)
        all_attn = gather_rows(grad_attn, ways)
        grad_attended = dot(all_attn, weight_out).astype(BF)
        grad_qkv = attention_call(
            attend_back_kernel, own, width, 3 * width, "attend_back", qkv, mask, grad_attended
        )
        first_terms = sum_rows(dot(grad_qkv, weight_qkv, NT), ways)
        normed_one, inverse_one = normalize(inputs)
        input_grad = grad_middle + norm_backward(
            first_terms, vector_rows[0], normed_one, inverse_one
        )

    with jax.named_scope("result"):
        down_terms = sum_rows(dot(active, weight_down, NT), ways)
        result = (middle + down_terms + vector_rows[7]).astype(BF)

    with jax.named_scope("attention_sums"):
        qkv_sums = jnp.sum(grad_qkv.astype(F32), axis=0)
        hidden_sums = jnp.sum(grad_hidden.astype(F32), axis=0)
        blank = jnp.zeros((D,), F32)
        vector_sums = jnp.stack(
            [
                jnp.sum(first_terms * normed_one, axis=0),
                jnp.sum(first_terms, axis=0),
                lax.dynamic_update_slice(blank, qkv_sums[:width], (me * width,)),
                lax.dynamic_update_slice(blank, qkv_sums[2 * width :], (me * width,)),
                jnp.sum(grad_attn.astype(F32), axis=0),
                jnp.sum(second_terms * normed_two, axis=0),
                jnp.sum(second_terms, axis=0),
                jnp.sum(grad_result, axis=0),
            ]
        )
        hidden_rows = lax.dynamic_update_slice(
            jnp.zeros((FF,), F32), hidden_sums, (me * hidden_width,)
        ).reshape(4, D)
        vector_sums = jnp.concatenate([vector_sums, hidden_rows], axis=0)
        attention_grads = jnp.concatenate(
            [
                dot(first_in, grad_qkv, TN),
                dot(all_attn, attended, TN),
                jnp.pad(vector_sums.T, ((0, 0), (0, VEC_PAD - vectors.shape[0]))),
            ],
            axis=1,
        )
        attention_total = lax.psum_scatter(attention_grads, "dp", scatter_dimension=0, tiled=True)

    with jax.named_scope("owners"):
        branch_parts = exchange(branch_total.reshape(ways, rows_own, -1))
        attention_parts = exchange(attention_total.reshape(ways, rows_own, -1))
        qkv_total = (
            attention_parts[:, :, : 3 * width]
            .reshape(ways, rows_own, 3, width)
            .transpose(1, 2, 0, 3)
            .reshape(rows_own, 3 * D)
        )
        reduced = (
            qkv_total,
            column_whole(attention_parts[:, :, 3 * width : 4 * width]),
            column_whole(branch_parts[:, :, :hidden_width]),
            column_whole(branch_parts[:, :, hidden_width:]),
            jnp.sum(attention_parts[:, :, 4 * width : 4 * width + vectors.shape[0]], axis=0).T,
        )
    states = (state_qkv, state_out, state_up, state_down, state_vectors)
    step_rates = (rate_matrix, rate_matrix, rate_matrix, rate_matrix, rate_vector)
    decay_rates = (decay_matrix, decay_matrix, decay_matrix, decay_matrix, 0.0)
    with jax.named_scope("adamw"):
        updates = [
            adamw(
                masters[place], reduced[place], states[place], step_rates[place], decay_rates[place]
            )
            for place in range(5)
        ]
    return (
        result,
        input_grad,
        *reduced,
        *(update[0] for update in updates),
        *(update[1] for update in updates),
    )


def solution(mesh):
    rows = P(("dp", "fsdp"), None)
    flat = P(("dp", "fsdp"))
    cols = P(None, ("dp", "fsdp"))
    moments = P(None, ("dp", "fsdp"), None)
    vector_moments = P(None, None, ("dp", "fsdp"))
    return jax.shard_map(
        functools.partial(per_device, mesh.shape["fsdp"]),
        mesh=mesh,
        in_specs=(
            rows, rows, flat, flat, rows, rows, rows, rows, cols,
            moments, moments, moments, moments, vector_moments,
        ),
        out_specs=(
            rows, rows, rows, rows, rows, rows, cols,
            moments, moments, moments, moments, vector_moments,
            rows, rows, rows, rows, cols,
        ),
        check_vma=False,
    )
```

```python
import functools

import jax
import jax.numpy as jnp
from jax import lax
from jax.experimental import pallas as pl
from jax.experimental.pallas import tpu as pltpu
from jax.sharding import PartitionSpec as P

D = 1024
HD = 64
FF = 4096
TILE = 32
TPM = 2
STEP = 10
BLOCK = TPM * TILE
EPS = 1e-05
VEC_PAD = 128
SCALE = HD**-0.5

rate_matrix = 0.06
rate_vector = 1.0
decay_matrix = 0.1

BF = jnp.bfloat16
F32 = jnp.float32
NN = (((1,), (0,)), ((), ()))
NT = (((1,), (1,)), ((), ()))
TN = (((0,), (0,)), ((), ()))


def dot(left, right, dims=NN):
    return lax.dot_general(left, right, dims, preferred_element_type=F32)


def normalize(values):
    centre = values - jnp.mean(values, axis=-1, keepdims=True)
    spread = jnp.mean(centre * centre, axis=-1, keepdims=True)
    inverse = lax.rsqrt(spread + EPS)
    return centre * inverse, inverse


def norm_backward(grads, gain, normed, inverse):
    scaled = grads * gain
    return inverse * (
        scaled
        - jnp.mean(scaled, axis=-1, keepdims=True)
        - normed * jnp.mean(scaled * normed, axis=-1, keepdims=True)
    )


def gelu_and_slope(values):
    root = (2.0 / jnp.pi) ** 0.5
    square = values * values
    bent = jnp.tanh(root * values * (1.0 + 0.044715 * square))
    half = 0.5 * (1.0 + bent)
    slope = half + 0.5 * values * (1.0 - bent * bent) * root * (1.0 + 3 * 0.044715 * square)
    return values * half, slope


def probabilities(query, key, mask):
    scores = jnp.where(mask, dot(query, key, NT) * SCALE, -1000000000.0)
    exp_scores = jnp.exp(scores - jnp.max(scores, axis=-1, keepdims=True))
    return exp_scores / jnp.sum(exp_scores, axis=-1, keepdims=True)


def attend_kernel(width, qkv_ref, mask_ref, out_ref):
    mask = mask_ref[...] > 0.5
    heads = []
    for at in range(0, width, HD):
        query = qkv_ref[:, at : at + HD]
        key = qkv_ref[:, width + at : width + at + HD]
        value = qkv_ref[:, 2 * width + at : 2 * width + at + HD]
        probs = probabilities(query, key, mask).astype(BF)
        heads.append(dot(probs, value))
    out_ref[...] = jnp.concatenate(heads, axis=1).astype(BF)


def attend_back_kernel(width, qkv_ref, mask_ref, grad_ref, out_ref):
    mask = mask_ref[...] > 0.5
    grad_q, grad_k, grad_v = [], [], []
    for at in range(0, width, HD):
        query = qkv_ref[:, at : at + HD]
        key = qkv_ref[:, width + at : width + at + HD]
        value = qkv_ref[:, 2 * width + at : 2 * width + at + HD]
        grad = grad_ref[:, at : at + HD]
        probs = probabilities(query, key, mask)
        grad_probs = dot(grad, value, NT)
        inner = jnp.sum(grad_probs * probs, axis=-1, keepdims=True)
        grad_scores = (probs * (grad_probs - inner)).astype(BF)
        grad_q.append(dot(grad_scores, key) * SCALE)
        grad_k.append(dot(grad_scores, query, TN) * SCALE)
        grad_v.append(dot(probs.astype(BF), grad, TN))
    out_ref[...] = jnp.concatenate(grad_q + grad_k + grad_v, axis=1).astype(BF)


def attention_call(kernel, own, width, out_width, name, *operands):
    total = operands[0].shape[0]
    return pl.pallas_call(
        functools.partial(kernel, width),
        grid=(total // own,),
        in_specs=[pl.BlockSpec((own, item.shape[1]), lambda i: (i, 0)) for item in operands],
        out_specs=pl.BlockSpec((own, out_width), lambda i: (i, 0)),
        out_shape=jax.ShapeDtypeStruct((total, out_width), BF),
        compiler_params=pltpu.CompilerParams(vmem_limit_bytes=32 * 1024 * 1024),
        name=name,
    )(*operands)


def row_codes(lengths, joins):
    per_block = joins.reshape(-1, TPM)
    sequence = jnp.cumsum(1 - per_block, axis=1)
    block = jnp.arange(per_block.shape[0], dtype=jnp.int32)[:, None]
    owner = (block * (TPM + 1) + sequence).reshape(-1)
    places = jnp.arange(TILE, dtype=jnp.int32)
    valid = (places[None, :] < lengths[:, None]).reshape(-1)
    codes = jnp.repeat(owner, TILE)
    rows = jnp.arange(codes.shape[0], dtype=jnp.int32)
    return valid, jnp.where(valid, codes, -1 - rows)


def gather_rows(values, ways):
    pieces = [values]
    for step in range(1, ways):
        order = [(place, (place + step) % ways) for place in range(ways)]
        pieces.append(lax.ppermute(values, "fsdp", order))
    return jnp.concatenate(pieces, axis=0)


def sum_rows(partial, ways):
    own = partial.shape[0] // ways
    total = partial[:own]
    for step in range(1, ways):
        order = [(place, (place - step) % ways) for place in range(ways)]
        piece = partial[step * own : (step + 1) * own].astype(BF)
        total = total + lax.ppermute(piece, "fsdp", order).astype(F32)
    return total


def exchange(values):
    return lax.all_to_all(values, "fsdp", split_axis=0, concat_axis=0, tiled=True)


def adamw(master, gradient, moments, step_rate, decay_rate):
    first_moment = 0.9 * moments[0] + 0.1 * gradient
    second_moment = 0.999 * moments[1] + 0.001 * gradient * gradient
    first_hat = first_moment / (1.0 - 0.9**STEP)
    second_hat = second_moment / (1.0 - 0.999**STEP)
    updated = master - step_rate * (
        first_hat / (jnp.sqrt(second_hat) + 1e-08) + decay_rate * master
    )
    return (jnp.stack([first_moment, second_moment]), updated)


def column_parts(weight, ways):
    rows = weight.shape[0]
    return weight.astype(BF).reshape(rows, ways, -1).transpose(1, 0, 2)


def column_whole(parts):
    return parts.transpose(1, 0, 2).reshape(parts.shape[1], -1)


def per_device(
    ways,
    tokens,
    cotangent,
    tile_len,
    tile_join,
    w_qkv,
    w_out,
    w_up,
    w_down,
    vectors,
    state_qkv,
    state_out,
    state_up,
    state_down,
    state_vectors,
):
    masters = (w_qkv, w_out, w_up, w_down, vectors)
    rows_own = w_qkv.shape[0]
    own = tokens.shape[0]
    width = D // ways
    hidden_width = FF // ways
    me = lax.axis_index("fsdp")

    with jax.named_scope("weights"):
        qkv_parts = (
            w_qkv.astype(BF).reshape(rows_own, 3, ways, width).transpose(2, 0, 1, 3)
        ).reshape(ways, rows_own, 3 * width)
        vector_part = jnp.pad(vectors.T, ((0, 0), (0, VEC_PAD - vectors.shape[0]))).astype(BF)
        first_payload = jnp.concatenate(
            [
                qkv_parts,
                column_parts(w_out, ways),
                jnp.broadcast_to(vector_part[None], (ways, rows_own, VEC_PAD)),
            ],
            axis=2,
        )
        second_payload = jnp.concatenate(
            [column_parts(w_up, ways), column_parts(w_down, ways)], axis=2
        )
        first_rows = exchange(first_payload).reshape(ways * rows_own, -1)
        first_weights = lax.all_gather(first_rows, "dp", axis=0, tiled=True)
        second_rows = exchange(second_payload).reshape(ways * rows_own, -1)
        second_weights = lax.all_gather(second_rows, "dp", axis=0, tiled=True)

    with jax.named_scope("rows"):
        valid, codes = row_codes(tile_len, tile_join)
        grad_branch = jnp.where(valid[:, None], cotangent, jnp.zeros_like(cotangent))
        all_tokens = gather_rows(tokens, ways)
        all_branch = gather_rows(grad_branch, ways)
        all_codes = gather_rows(codes, ways).reshape(ways, own)
        places = jnp.arange(own, dtype=jnp.int32)
        causal = places[:, None] >= places[None, :]
        mask = (all_codes[:, :, None] == all_codes[:, None, :]) & causal[None]
        mask = mask.astype(F32).reshape(ways * own, own)

    weight_qkv = first_weights[:, : 3 * width]
    weight_out = first_weights[:, 3 * width : 4 * width]
    vector_rows = first_weights[:, 4 * width : 4 * width + vectors.shape[0]].T.astype(F32)
    bias_query = lax.dynamic_slice(vector_rows[2], (me * width,), (width,))
    bias_value = lax.dynamic_slice(vector_rows[3], (me * width,), (width,))
    bias_qkv = jnp.concatenate([bias_query, jnp.zeros_like(bias_query), bias_value])
    bias_up = lax.dynamic_slice(
        vector_rows[8:12].reshape(-1), (me * hidden_width,), (hidden_width,)
    )

    with jax.named_scope("forward"):
        inputs = tokens.astype(F32)
        all_normed, _ = normalize(all_tokens.astype(F32))
        first_in = (all_normed * vector_rows[0] + vector_rows[1]).astype(BF)
        qkv = (dot(first_in, weight_qkv) + bias_qkv).astype(BF)
        attended = attention_call(attend_kernel, own, width, width, "attend", qkv, mask)
        out_terms = sum_rows(dot(attended, weight_out, NT), ways)
        middle = inputs + out_terms + vector_rows[4]
        normed_two, inverse_two = normalize(middle)
        second_own = (normed_two * vector_rows[5] + vector_rows[6]).astype(BF)
        second_in = gather_rows(second_own, ways)

    weight_up = second_weights[:, :hidden_width]
    weight_down = second_weights[:, hidden_width:]

    with jax.named_scope("branch"):
        hidden = dot(second_in, weight_up) + bias_up
        active, slope = gelu_and_slope(hidden)
        active = active.astype(BF)
        grad_hidden = (dot(all_branch, weight_down) * slope).astype(BF)
        second_terms = sum_rows(dot(grad_hidden, weight_up, NT), ways)

    with jax.named_scope("branch_sums"):
        branch_grads = jnp.concatenate(
            [dot(second_in, grad_hidden, TN).astype(BF), dot(all_branch, active, TN).astype(BF)],
            axis=1,
        )
        branch_grads, second_terms = lax.optimization_barrier((branch_grads, second_terms))
        branch_total = lax.psum_scatter(branch_grads, "dp", scatter_dimension=0, tiled=True)

    with jax.named_scope("backward"):
        grad_result = grad_branch.astype(F32)
        grad_middle = grad_result + norm_backward(
            second_terms, vector_rows[5], normed_two, inverse_two
        )
        grad_attn = grad_middle.astype(BF)
        all_attn = gather_rows(grad_attn, ways)
        grad_attended = dot(all_attn, weight_out).astype(BF)
        grad_qkv = attention_call(
            attend_back_kernel, own, width, 3 * width, "attend_back", qkv, mask, grad_attended
        )
        first_terms = sum_rows(dot(grad_qkv, weight_qkv, NT), ways)
        normed_one, inverse_one = normalize(inputs)
        input_grad = grad_middle + norm_backward(
            first_terms, vector_rows[0], normed_one, inverse_one
        )

    with jax.named_scope("result"):
        down_terms = sum_rows(dot(active, weight_down, NT), ways)
        result = (middle + down_terms + vector_rows[7]).astype(BF)

    with jax.named_scope("attention_sums"):
        qkv_sums = jnp.sum(grad_qkv.astype(F32), axis=0)
        hidden_sums = jnp.sum(grad_hidden.astype(F32), axis=0)
        blank = jnp.zeros((D,), F32)
        vector_sums = jnp.stack(
            [
                jnp.sum(first_terms * normed_one, axis=0),
                jnp.sum(first_terms, axis=0),
                lax.dynamic_update_slice(blank, qkv_sums[:width], (me * width,)),
                lax.dynamic_update_slice(blank, qkv_sums[2 * width :], (me * width,)),
                jnp.sum(grad_attn.astype(F32), axis=0),
                jnp.sum(second_terms * normed_two, axis=0),
                jnp.sum(second_terms, axis=0),
                jnp.sum(grad_result, axis=0),
            ]
        )
        hidden_rows = lax.dynamic_update_slice(
            jnp.zeros((FF,), F32), hidden_sums, (me * hidden_width,)
        ).reshape(4, D)
        vector_sums = jnp.concatenate([vector_sums, hidden_rows], axis=0)
        attention_grads = jnp.concatenate(
            [
                dot(first_in, grad_qkv, TN).astype(BF),
                dot(all_attn, attended, TN).astype(BF),
                jnp.pad(vector_sums.T, ((0, 0), (0, VEC_PAD - vectors.shape[0]))).astype(BF),
            ],
            axis=1,
        )
        attention_grads, branch_total = lax.optimization_barrier((attention_grads, branch_total))
        attention_total = lax.psum_scatter(attention_grads, "dp", scatter_dimension=0, tiled=True)

    with jax.named_scope("owners"):
        branch_parts = exchange(branch_total.reshape(ways, rows_own, -1)).astype(F32)
        attention_parts = exchange(attention_total.reshape(ways, rows_own, -1)).astype(F32)
        qkv_total = (
            attention_parts[:, :, : 3 * width]
            .reshape(ways, rows_own, 3, width)
            .transpose(1, 2, 0, 3)
            .reshape(rows_own, 3 * D)
        )
        reduced = (
            qkv_total,
            column_whole(attention_parts[:, :, 3 * width : 4 * width]),
            column_whole(branch_parts[:, :, :hidden_width]),
            column_whole(branch_parts[:, :, hidden_width:]),
            jnp.sum(attention_parts[:, :, 4 * width : 4 * width + vectors.shape[0]], axis=0).T,
        )
    states = (state_qkv, state_out, state_up, state_down, state_vectors)
    step_rates = (rate_matrix, rate_matrix, rate_matrix, rate_matrix, rate_vector)
    decay_rates = (decay_matrix, decay_matrix, decay_matrix, decay_matrix, 0.0)
    with jax.named_scope("adamw"):
        updates = [
            adamw(
                masters[place], reduced[place], states[place], step_rates[place], decay_rates[place]
            )
            for place in range(5)
        ]
    return (
        result,
        input_grad,
        *reduced,
        *(update[0] for update in updates),
        *(update[1] for update in updates),
    )


def solution(mesh):
    rows = P(("dp", "fsdp"), None)
    flat = P(("dp", "fsdp"))
    cols = P(None, ("dp", "fsdp"))
    moments = P(None, ("dp", "fsdp"), None)
    vector_moments = P(None, None, ("dp", "fsdp"))
    return jax.shard_map(
        functools.partial(per_device, mesh.shape["fsdp"]),
        mesh=mesh,
        in_specs=(
            rows, rows, flat, flat, rows, rows, rows, rows, cols,
            moments, moments, moments, moments, vector_moments,
        ),
        out_specs=(
            rows, rows, rows, rows, rows, rows, cols,
            moments, moments, moments, moments, vector_moments,
            rows, rows, rows, rows, cols,
        ),
        check_vma=False,
    )
```

```python
import functools

import jax
import jax.numpy as jnp
from jax import lax
from jax.experimental import pallas as pl
from jax.experimental.pallas import tpu as pltpu
from jax.sharding import PartitionSpec as P

D = 1024
HD = 64
FF = 4096
TILE = 32
TPM = 2
STEP = 10
BLOCK = TPM * TILE
EPS = 1e-05
VEC_PAD = 128
SCALE = HD**-0.5

rate_matrix = 0.06
rate_vector = 1.0
decay_matrix = 0.1

BF = jnp.bfloat16
F32 = jnp.float32
NN = (((1,), (0,)), ((), ()))
NT = (((1,), (1,)), ((), ()))
TN = (((0,), (0,)), ((), ()))


def dot(left, right, dims=NN):
    return lax.dot_general(left, right, dims, preferred_element_type=F32)


def normalize(values):
    centre = values - jnp.mean(values, axis=-1, keepdims=True)
    spread = jnp.mean(centre * centre, axis=-1, keepdims=True)
    inverse = lax.rsqrt(spread + EPS)
    return centre * inverse, inverse


def norm_backward(grads, gain, normed, inverse):
    scaled = grads * gain
    return inverse * (
        scaled
        - jnp.mean(scaled, axis=-1, keepdims=True)
        - normed * jnp.mean(scaled * normed, axis=-1, keepdims=True)
    )


def gelu_and_slope(values):
    root = (2.0 / jnp.pi) ** 0.5
    square = values * values
    bent = jnp.tanh(root * values * (1.0 + 0.044715 * square))
    half = 0.5 * (1.0 + bent)
    slope = half + 0.5 * values * (1.0 - bent * bent) * root * (1.0 + 3 * 0.044715 * square)
    return values * half, slope


def probabilities(query, key, mask):
    scores = jnp.where(mask, dot(query, key, NT) * SCALE, -1000000000.0)
    exp_scores = jnp.exp(scores - jnp.max(scores, axis=-1, keepdims=True))
    return exp_scores / jnp.sum(exp_scores, axis=-1, keepdims=True)


def attend_kernel(width, qkv_ref, mask_ref, out_ref):
    mask = mask_ref[...] > 0.5
    heads = []
    for at in range(0, width, HD):
        query = qkv_ref[:, at : at + HD]
        key = qkv_ref[:, width + at : width + at + HD]
        value = qkv_ref[:, 2 * width + at : 2 * width + at + HD]
        probs = probabilities(query, key, mask).astype(BF)
        heads.append(dot(probs, value))
    out_ref[...] = jnp.concatenate(heads, axis=1).astype(BF)


def attend_back_kernel(width, qkv_ref, mask_ref, grad_ref, out_ref):
    mask = mask_ref[...] > 0.5
    grad_q, grad_k, grad_v = [], [], []
    for at in range(0, width, HD):
        query = qkv_ref[:, at : at + HD]
        key = qkv_ref[:, width + at : width + at + HD]
        value = qkv_ref[:, 2 * width + at : 2 * width + at + HD]
        grad = grad_ref[:, at : at + HD]
        probs = probabilities(query, key, mask)
        grad_probs = dot(grad, value, NT)
        inner = jnp.sum(grad_probs * probs, axis=-1, keepdims=True)
        grad_scores = (probs * (grad_probs - inner)).astype(BF)
        grad_q.append(dot(grad_scores, key) * SCALE)
        grad_k.append(dot(grad_scores, query, TN) * SCALE)
        grad_v.append(dot(probs.astype(BF), grad, TN))
    out_ref[...] = jnp.concatenate(grad_q + grad_k + grad_v, axis=1).astype(BF)


def attention_call(kernel, own, width, out_width, name, *operands):
    total = operands[0].shape[0]
    return pl.pallas_call(
        functools.partial(kernel, width),
        grid=(total // own,),
        in_specs=[pl.BlockSpec((own, item.shape[1]), lambda i: (i, 0)) for item in operands],
        out_specs=pl.BlockSpec((own, out_width), lambda i: (i, 0)),
        out_shape=jax.ShapeDtypeStruct((total, out_width), BF),
        compiler_params=pltpu.CompilerParams(vmem_limit_bytes=32 * 1024 * 1024),
        name=name,
    )(*operands)


def row_codes(lengths, joins):
    per_block = joins.reshape(-1, TPM)
    sequence = jnp.cumsum(1 - per_block, axis=1)
    block = jnp.arange(per_block.shape[0], dtype=jnp.int32)[:, None]
    owner = (block * (TPM + 1) + sequence).reshape(-1)
    places = jnp.arange(TILE, dtype=jnp.int32)
    valid = (places[None, :] < lengths[:, None]).reshape(-1)
    codes = jnp.repeat(owner, TILE)
    rows = jnp.arange(codes.shape[0], dtype=jnp.int32)
    return valid, jnp.where(valid, codes, -1 - rows)


def gather_rows(values, ways):
    pieces = [values]
    for step in range(1, ways):
        order = [(place, (place + step) % ways) for place in range(ways)]
        pieces.append(lax.ppermute(values, "fsdp", order))
    return jnp.concatenate(pieces, axis=0)


def sum_rows(partial, ways):
    own = partial.shape[0] // ways
    total = partial[:own]
    for step in range(1, ways):
        order = [(place, (place - step) % ways) for place in range(ways)]
        piece = partial[step * own : (step + 1) * own].astype(BF)
        total = total + lax.ppermute(piece, "fsdp", order).astype(F32)
    return total


def exchange(values):
    return lax.all_to_all(values, "fsdp", split_axis=0, concat_axis=0, tiled=True)


def swapped(values, bit, count):
    order = [(place, place ^ (1 << bit)) for place in range(count)]
    return lax.ppermute(values, "dp", order)


def sum_halving(terms, order, count):
    left = list(range(len(order)))
    for bit in order:
        before = sum(other > bit for other in left)
        view = terms.reshape(2**before, 2, -1, terms.shape[-1])
        upper = ((lax.axis_index("dp") >> bit) & 1) == 1
        kept = jnp.where(upper, view[:, 1], view[:, 0])
        sent = jnp.where(upper, view[:, 0], view[:, 1]).astype(BF)
        terms = kept + swapped(sent, bit, count).astype(F32)
        left.remove(bit)
    return terms.reshape(-1, terms.shape[-1])


def gather_doubling(values, order, count):
    held = []
    for bit in order:
        before = sum(other > bit for other in held)
        other_half = swapped(values, bit, count)
        upper = ((lax.axis_index("dp") >> bit) & 1) == 1
        halves = (jnp.where(upper, other_half, values), jnp.where(upper, values, other_half))
        halves = [half.reshape(2**before, 1, -1, half.shape[-1]) for half in halves]
        values = jnp.concatenate(halves, axis=1).reshape(-1, values.shape[-1])
        held.append(bit)
    return values


def adamw(master, gradient, moments, step_rate, decay_rate):
    first_moment = 0.9 * moments[0] + 0.1 * gradient
    second_moment = 0.999 * moments[1] + 0.001 * gradient * gradient
    first_hat = first_moment / (1.0 - 0.9**STEP)
    second_hat = second_moment / (1.0 - 0.999**STEP)
    updated = master - step_rate * (
        first_hat / (jnp.sqrt(second_hat) + 1e-08) + decay_rate * master
    )
    return (jnp.stack([first_moment, second_moment]), updated)


def column_parts(weight, ways):
    rows = weight.shape[0]
    return weight.astype(BF).reshape(rows, ways, -1).transpose(1, 0, 2)


def column_whole(parts):
    return parts.transpose(1, 0, 2).reshape(parts.shape[1], -1)


def per_device(
    ways,
    count,
    tokens,
    cotangent,
    tile_len,
    tile_join,
    w_qkv,
    w_out,
    w_up,
    w_down,
    vectors,
    state_qkv,
    state_out,
    state_up,
    state_down,
    state_vectors,
):
    masters = (w_qkv, w_out, w_up, w_down, vectors)
    rows_own = w_qkv.shape[0]
    own = tokens.shape[0]
    width = D // ways
    hidden_width = FF // ways
    me = lax.axis_index("fsdp")

    with jax.named_scope("weights"):
        qkv_parts = (
            w_qkv.astype(BF).reshape(rows_own, 3, ways, width).transpose(2, 0, 1, 3)
        ).reshape(ways, rows_own, 3 * width)
        vector_part = jnp.pad(vectors.T, ((0, 0), (0, VEC_PAD - vectors.shape[0]))).astype(BF)
        first_payload = jnp.concatenate(
            [
                qkv_parts,
                column_parts(w_out, ways),
                jnp.broadcast_to(vector_part[None], (ways, rows_own, VEC_PAD)),
            ],
            axis=2,
        )
        second_payload = jnp.concatenate(
            [column_parts(w_up, ways), column_parts(w_down, ways)], axis=2
        )
        first_rows = exchange(first_payload).reshape(ways * rows_own, -1)
        second_rows = exchange(second_payload).reshape(ways * rows_own, -1)
        second_weights = lax.all_gather(second_rows, "dp", axis=0, tiled=True)
        bits = list(range(count.bit_length() - 1))
        turned = bits[1:] + bits[:1]
        weight_qkv = gather_doubling(first_rows[:, : 3 * width], bits[::-1], count)
        out_and_vectors = gather_doubling(first_rows[:, 3 * width :], turned[::-1], count)

    with jax.named_scope("rows"):
        valid, codes = row_codes(tile_len, tile_join)
        grad_branch = jnp.where(valid[:, None], cotangent, jnp.zeros_like(cotangent))
        all_tokens = gather_rows(tokens, ways)
        all_branch = gather_rows(grad_branch, ways)
        all_codes = gather_rows(codes, ways).reshape(ways, own)
        places = jnp.arange(own, dtype=jnp.int32)
        causal = places[:, None] >= places[None, :]
        mask = (all_codes[:, :, None] == all_codes[:, None, :]) & causal[None]
        mask = mask.astype(F32).reshape(ways * own, own)

    weight_out = out_and_vectors[:, :width]
    vector_rows = out_and_vectors[:, width : width + vectors.shape[0]].T.astype(F32)
    bias_query = lax.dynamic_slice(vector_rows[2], (me * width,), (width,))
    bias_value = lax.dynamic_slice(vector_rows[3], (me * width,), (width,))
    bias_qkv = jnp.concatenate([bias_query, jnp.zeros_like(bias_query), bias_value])
    bias_up = lax.dynamic_slice(
        vector_rows[8:12].reshape(-1), (me * hidden_width,), (hidden_width,)
    )

    with jax.named_scope("forward"):
        inputs = tokens.astype(F32)
        all_normed, _ = normalize(all_tokens.astype(F32))
        first_in = (all_normed * vector_rows[0] + vector_rows[1]).astype(BF)
        qkv = (dot(first_in, weight_qkv) + bias_qkv).astype(BF)
        attended = attention_call(attend_kernel, own, width, width, "attend", qkv, mask)
        out_terms = sum_rows(dot(attended, weight_out, NT), ways)
        middle = inputs + out_terms + vector_rows[4]
        normed_two, inverse_two = normalize(middle)
        second_own = (normed_two * vector_rows[5] + vector_rows[6]).astype(BF)
        second_in = gather_rows(second_own, ways)

    weight_up = second_weights[:, :hidden_width]
    weight_down = second_weights[:, hidden_width:]

    with jax.named_scope("branch"):
        hidden = dot(second_in, weight_up) + bias_up
        active, slope = gelu_and_slope(hidden)
        active = active.astype(BF)
        grad_hidden = (dot(all_branch, weight_down) * slope).astype(BF)
        second_terms = sum_rows(dot(grad_hidden, weight_up, NT), ways)

    with jax.named_scope("branch_sums"):
        branch_grads = jnp.concatenate(
            [dot(second_in, grad_hidden, TN).astype(BF), dot(all_branch, active, TN).astype(BF)],
            axis=1,
        )
        branch_grads, second_terms = lax.optimization_barrier((branch_grads, second_terms))
        branch_total = lax.psum_scatter(branch_grads, "dp", scatter_dimension=0, tiled=True)

    with jax.named_scope("backward"):
        grad_result = grad_branch.astype(F32)
        grad_middle = grad_result + norm_backward(
            second_terms, vector_rows[5], normed_two, inverse_two
        )
        grad_attn = grad_middle.astype(BF)
        all_attn = gather_rows(grad_attn, ways)
        grad_attended = dot(all_attn, weight_out).astype(BF)
        grad_qkv = attention_call(
            attend_back_kernel, own, width, 3 * width, "attend_back", qkv, mask, grad_attended
        )
        first_terms = sum_rows(dot(grad_qkv, weight_qkv, NT), ways)
        normed_one, inverse_one = normalize(inputs)
        input_grad = grad_middle + norm_backward(
            first_terms, vector_rows[0], normed_one, inverse_one
        )

    with jax.named_scope("result"):
        down_terms = sum_rows(dot(active, weight_down, NT), ways)
        result = (middle + down_terms + vector_rows[7]).astype(BF)

    with jax.named_scope("attention_sums"):
        qkv_sums = jnp.sum(grad_qkv.astype(F32), axis=0)
        hidden_sums = jnp.sum(grad_hidden.astype(F32), axis=0)
        blank = jnp.zeros((D,), F32)
        vector_sums = jnp.stack(
            [
                jnp.sum(first_terms * normed_one, axis=0),
                jnp.sum(first_terms, axis=0),
                lax.dynamic_update_slice(blank, qkv_sums[:width], (me * width,)),
                lax.dynamic_update_slice(blank, qkv_sums[2 * width :], (me * width,)),
                jnp.sum(grad_attn.astype(F32), axis=0),
                jnp.sum(second_terms * normed_two, axis=0),
                jnp.sum(second_terms, axis=0),
                jnp.sum(grad_result, axis=0),
            ]
        )
        hidden_rows = lax.dynamic_update_slice(
            jnp.zeros((FF,), F32), hidden_sums, (me * hidden_width,)
        ).reshape(4, D)
        vector_sums = jnp.concatenate([vector_sums, hidden_rows], axis=0)
        qkv_own = sum_halving(dot(first_in, grad_qkv, TN), bits, count)
        out_grads = jnp.concatenate(
            [
                dot(all_attn, attended, TN),
                jnp.pad(vector_sums.T, ((0, 0), (0, VEC_PAD - vectors.shape[0]))),
            ],
            axis=1,
        )
        out_own = sum_halving(out_grads, turned, count)
        attention_total = jnp.concatenate([qkv_own, out_own], axis=1).astype(BF)
        attention_total, branch_total = lax.optimization_barrier((attention_total, branch_total))

    with jax.named_scope("owners"):
        branch_parts = exchange(branch_total.reshape(ways, rows_own, -1)).astype(F32)
        attention_parts = exchange(attention_total.reshape(ways, rows_own, -1)).astype(F32)
        qkv_total = (
            attention_parts[:, :, : 3 * width]
            .reshape(ways, rows_own, 3, width)
            .transpose(1, 2, 0, 3)
            .reshape(rows_own, 3 * D)
        )
        reduced = (
            qkv_total,
            column_whole(attention_parts[:, :, 3 * width : 4 * width]),
            column_whole(branch_parts[:, :, :hidden_width]),
            column_whole(branch_parts[:, :, hidden_width:]),
            jnp.sum(attention_parts[:, :, 4 * width : 4 * width + vectors.shape[0]], axis=0).T,
        )
    states = (state_qkv, state_out, state_up, state_down, state_vectors)
    step_rates = (rate_matrix, rate_matrix, rate_matrix, rate_matrix, rate_vector)
    decay_rates = (decay_matrix, decay_matrix, decay_matrix, decay_matrix, 0.0)
    with jax.named_scope("adamw"):
        updates = [
            adamw(
                masters[place], reduced[place], states[place], step_rates[place], decay_rates[place]
            )
            for place in range(5)
        ]
    return (
        result,
        input_grad,
        *reduced,
        *(update[0] for update in updates),
        *(update[1] for update in updates),
    )


def solution(mesh):
    rows = P(("dp", "fsdp"), None)
    flat = P(("dp", "fsdp"))
    cols = P(None, ("dp", "fsdp"))
    moments = P(None, ("dp", "fsdp"), None)
    vector_moments = P(None, None, ("dp", "fsdp"))
    return jax.shard_map(
        functools.partial(per_device, mesh.shape["fsdp"], mesh.shape["dp"]),
        mesh=mesh,
        in_specs=(
            rows, rows, flat, flat, rows, rows, rows, rows, cols,
            moments, moments, moments, moments, vector_moments,
        ),
        out_specs=(
            rows, rows, rows, rows, rows, rows, cols,
            moments, moments, moments, moments, vector_moments,
            rows, rows, rows, rows, cols,
        ),
        check_vma=False,
    )
```
